32 devices in a mesh: node: 8 (over z, y), local: 4 (over x, core).
Axes of the slice: x: 2, y: 2, z: 4, core: 2. Of those that a mesh axis runs over, the one named last changes fastest.
Arguments:
- tokens: bfloat16 [4096, 7168], P(('node', 'local')), may hold values from -6 to 6
- out_grad: bfloat16 [4096, 7168], P(('node', 'local')), may hold values from -6 to 6
- route_ids: int32 [4096, 1], P(('node', 'local')), may hold values from 0 to 7; in each aligned block of 128 rows (0 to 127, 128 to 255, ...) at most 24 rows name the same one
- route_weights: bfloat16 [4096, 1], P(('node', 'local')), may hold values from 0.049804688 to 1
- gate_proj: bfloat16 [8, 7168, 2048], P('node', None, 'local'), may hold values from -0.0625 to 0.0625
- up_proj: bfloat16 [8, 7168, 2048], P('node', None, 'local'), may hold values from -0.0625 to 0.0625
- down_proj: bfloat16 [8, 2048, 7168], P('node', 'local'), may hold values from -0.125 to 0.125
Outputs:
- grad_tokens: bfloat16 [4096, 7168], P(('node', 'local'))
- grad_routes: float32 [4096, 1], P(('node', 'local'))
- grad_gate: bfloat16 [8, 7168, 2048], P('node', None, 'local')
- grad_up: bfloat16 [8, 7168, 2048], P('node', None, 'local')
- grad_down: bfloat16 [8, 2048, 7168], P('node', 'local')
The draws below stay inside these ranges and needn't reach their ends.
Inputs may be any that keep to these rules, and one draw needn't show every extreme that they name: `route_ids`: the 1 ids of a token are distinct; among the 128 tokens of one block no id appears more than 24 times, and in every draw some block names some id exactly 24 times. Every id is named somewhere.
All inputs are finite; a program needn't handle non-finite values.
Results may differ from the reference program's by a relative error of at most 0.0095.
Values may be sent and summed in bfloat16 or wider, within the bound.
A program may use at most 384 MiB of HBM per device.

```python
import math
import jax
import jax.numpy as jnp
import numpy as np
from jax import lax

D = 7168
FF = 2048
TOPK = 1
TOK_DEV = 128
EXPERTS = 8
BLOCKS = 32
TOKENS = 4096
CAP = 24
SLOTS = 768
FF_DEV = 512
N_LOCAL = 4


def level_of(rng, shape, cuts, smallest, largest):
    def one(position, parts):
        draws = jax.random.uniform(jax.random.fold_in(jax.random.fold_in(rng, 6), position), (parts,), jnp.float32, smallest / len(cuts), largest / len(cuts))
        return jnp.repeat(jnp.exp(draws), shape[position] // parts).reshape((-1,) + (1,) * (len(shape) - position - 1))

    loudness = one(*cuts[0])
    for cut in cuts[1:]:
        loudness = loudness * one(*cut)
    return loudness


def routed_block(own_key, own, number, rows, number_of, top, reach, lean):
    order = jax.random.permutation(own_key, number_of)
    packed, usual = load_shares(number_of, rows * top, reach, lean, True), load_shares(number_of, rows * top, reach, lean, False)
    places = jnp.arange(number_of)

    def named(tallies, offset_by):
        used = int((tallies > 0).sum())
        fixed = max(1, used // 4)
        passed = fixed + (places - fixed + offset_by * (used - fixed)) % max(1, number_of - fixed)
        return jnp.zeros((number_of,), jnp.int32).at[order[jnp.where(places < fixed, places, passed)]].set(jnp.asarray(tallies, jnp.int32))

    tallies = jnp.where(number % 4 == 0, named(packed, number // 4), named(usual, number - number // 4 - 1))
    mixed = jax.random.permutation(jax.random.fold_in(own, 3), number_of)
    giver, receiver = mixed[0:number_of // 2 * 2:2], mixed[1:number_of // 2 * 2:2]
    slack = jnp.minimum(tallies[giver] - 1, reach - tallies[receiver]) // 2
    slack = jnp.where((giver == order[0]) | (receiver == order[0]) | (tallies[receiver] == 0), 0, jnp.maximum(slack, 0))
    passed = jax.random.randint(jax.random.fold_in(own, 4), (number_of // 2,), 0, 1 << 20) % (slack + 1)
    tallies = tallies.at[giver].add(-passed).at[receiver].add(passed)
    labels = jnp.searchsorted(jnp.cumsum(tallies), jnp.arange(rows * top), side="right").astype(jnp.int32)
    grid = labels.reshape(top, rows).T
    grid = grid[jax.random.permutation(jax.random.fold_in(own, 1), rows)]
    offset_by = jax.random.randint(jax.random.fold_in(own, 2), (rows, 1), 0, top)
    return jnp.take_along_axis(grid, (jnp.arange(top)[None, :] + offset_by) % top, axis=1)


def load_shares(amount, total, most, lean, full):
    loads = [(1 << 20) // math.isqrt(standing ** lean) + 1 for standing in range(1, amount + 1)]
    largest = most if full else min(most, max(-(-total // amount), total * loads[0] // sum(loads)))
    least = 1 if total - largest >= amount - 1 else 0
    given, rest = [largest] + [least] * (amount - 1), total - largest - least * (amount - 1)
    while rest > 0:
        candidates = [i for i in range(1, amount) if given[i] < largest] or [i for i in range(1, amount) if given[i] < most]
        mass, remaining = sum([loads[i] for i in candidates]), rest
        for i in candidates:
            addition = min(most - given[i], max(1, remaining * loads[i] // mass), rest)
            given[i] = given[i] + addition
            rest = rest - addition
    return np.array(given)


def normal_values(stream_key, shape, deviation, reach, cuts=(), kind=jnp.bfloat16):
    drawn = jax.random.normal(stream_key, shape, jnp.float32) * deviation
    if len(cuts) > 0:
        drawn = level_of(stream_key, shape, cuts, -0.22, 0.18) * drawn
    return jnp.clip(drawn, min=-reach, max=reach).astype(kind)


def setup_inputs(seed: int = 0) -> dict:
    streams_of = jax.random.split(jax.random.key(seed), 8)
    tokens = normal_values(streams_of[0], (TOKENS, D), 1.0, 6.0, ((0, 32),))
    out_grad = normal_values(streams_of[1], (TOKENS, D), 1.0, 6.0, ((0, 32),))
    route_ids_keys = jax.random.split(jax.random.fold_in(streams_of[2], 1), TOKENS // TOK_DEV)
    route_ids_turns = jax.random.permutation(jax.random.fold_in(streams_of[2], 3), TOKENS // TOK_DEV)
    route_ids = jax.vmap(lambda own, number: routed_block(jax.random.fold_in(streams_of[2], 2), own, number, TOK_DEV, EXPERTS, TOPK, CAP, 2))(route_ids_keys, route_ids_turns).reshape((TOKENS, TOPK))
    route_weights = jnp.clip(jnp.exp(math.log(1.0) - 2.9996462 * jax.random.uniform(streams_of[3], (TOKENS, TOPK), jnp.float32) ** level_of(streams_of[3], (TOKENS, TOPK), ((0, 32),), -0.2, 0.2)), 0.049804688, 1.0).astype(jnp.bfloat16)
    gate_proj = normal_values(streams_of[4], (EXPERTS, D, FF), D ** -0.5, 0.0625, ((0, 8), (2, 4)))
    up_proj = normal_values(streams_of[5], (EXPERTS, D, FF), D ** -0.5, 0.0625, ((0, 8), (2, 4)))
    down_proj = normal_values(streams_of[6], (EXPERTS, FF, D), FF ** -0.5, 0.125, ((0, 8), (1, 4)))
    return dict(tokens=tokens, out_grad=out_grad, route_ids=route_ids, route_weights=route_weights, gate_proj=gate_proj, up_proj=up_proj, down_proj=down_proj)


def expert_grads(operands):
    rows_x, rows_dy, rows_g, gate_w, up_w, down_w = operands
    pre_gate = jnp.dot(rows_x, gate_w, preferred_element_type=jnp.float32)
    pre_up = jnp.dot(rows_x, up_w, preferred_element_type=jnp.float32)
    gate_sigmoid = jax.nn.sigmoid(pre_gate)
    gate_silu = pre_gate * gate_sigmoid
    activated = (gate_silu * pre_up).astype(jnp.bfloat16)
    back_proj = jnp.dot(rows_dy, down_w.T, preferred_element_type=jnp.float32)
    gate_scale = rows_g.astype(jnp.float32)[:, None]
    grad_act = gate_scale * back_proj
    grad_pregate = (grad_act * pre_up * gate_sigmoid * (1.0 + pre_gate * (1.0 - gate_sigmoid))).astype(jnp.bfloat16)
    grad_preup = (grad_act * gate_silu).astype(jnp.bfloat16)
    scaled = (gate_scale * rows_dy.astype(jnp.float32)).astype(jnp.bfloat16)
    grad_gate = jnp.dot(rows_x.T, grad_pregate, preferred_element_type=jnp.float32).astype(jnp.bfloat16)
    grad_up = jnp.dot(rows_x.T, grad_preup, preferred_element_type=jnp.float32).astype(jnp.bfloat16)
    grad_down = jnp.dot(activated.T, scaled, preferred_element_type=jnp.float32).astype(jnp.bfloat16)
    product = activated.astype(jnp.float32) * back_proj
    row_grad = jnp.zeros((SLOTS, D), jnp.float32)
    row_weight = jnp.zeros((SLOTS,), jnp.float32)
    for slice_id in range(N_LOCAL):
        low = slice_id * FF_DEV
        high = low + FF_DEV
        part_x = jnp.dot(grad_pregate[:, low:high], gate_w[:, low:high].T, preferred_element_type=jnp.float32)
        part_x = part_x + jnp.dot(grad_preup[:, low:high], up_w[:, low:high].T, preferred_element_type=jnp.float32)
        part_x = lax.optimization_barrier(part_x.astype(jnp.bfloat16))
        row_grad = row_grad + part_x.astype(jnp.float32)
        part_g = lax.optimization_barrier(jnp.sum(product[:, low:high], axis=1).astype(jnp.bfloat16))
        row_weight = row_weight + part_g.astype(jnp.float32)
    return row_grad, row_weight, grad_gate, grad_up, grad_down


def reference(tokens, out_grad, route_ids, route_weights, gate_proj, up_proj, down_proj):
    per_block = TOK_DEV * TOPK
    flat_ids = route_ids.reshape(BLOCKS, per_block).astype(jnp.int32)
    route_order = jnp.arange(per_block, dtype=jnp.int32)
    earlier = route_order[None, :] < route_order[:, None]
    same_ids = (flat_ids[:, :, None] == flat_ids[:, None, :]) & earlier[None, :, :]
    rank_ids = jnp.sum(same_ids.astype(jnp.int32), axis=2)
    block_ids = jnp.arange(BLOCKS, dtype=jnp.int32)[:, None]
    slot_index = (flat_ids * SLOTS + block_ids * CAP + rank_ids).reshape(-1).astype(jnp.int32)
    token_of = (jnp.arange(TOKENS * TOPK, dtype=jnp.int32) // TOPK).astype(jnp.int32)
    buffer_x = jnp.zeros((EXPERTS * SLOTS, D), tokens.dtype).at[slot_index].set(tokens[token_of])
    buffer_dy = jnp.zeros((EXPERTS * SLOTS, D), out_grad.dtype).at[slot_index].set(out_grad[token_of])
    buffer_g = jnp.zeros((EXPERTS * SLOTS,), route_weights.dtype).at[slot_index].set(route_weights.reshape(-1))
    row_grad, row_weight, grad_gate, grad_up, grad_down = lax.map(
        expert_grads,
        (buffer_x.reshape(EXPERTS, SLOTS, D), buffer_dy.reshape(EXPERTS, SLOTS, D),
         buffer_g.reshape(EXPERTS, SLOTS), gate_proj, up_proj, down_proj))
    route_rows = row_grad.reshape(EXPERTS * SLOTS, D)[slot_index]
    grad_tokens = jnp.sum(route_rows.reshape(TOKENS, TOPK, D), axis=1).astype(jnp.bfloat16)
    grad_routes = row_weight.reshape(EXPERTS * SLOTS)[slot_index].reshape(TOKENS, TOPK)
    return grad_tokens, grad_routes, grad_gate, grad_up, grad_down
```

```python
import jax
import jax.numpy as jnp
from jax import lax
from jax.sharding import PartitionSpec as P

IN_PARTS = 2
OUT_PARTS = 2


def slot_tables(route_ids, experts, capacity):
    tok_count, top_count = route_ids.shape
    flat_ids = route_ids.reshape(tok_count * top_count)
    route_order = jnp.arange(tok_count * top_count, dtype=jnp.int32)
    same_ids = (flat_ids[:, None] == flat_ids[None, :]) & (
        route_order[None, :] < route_order[:, None]
    )
    rank_ids = jnp.sum(same_ids.astype(jnp.int32), axis=1)
    slot_index = flat_ids * capacity + rank_ids
    slot_lines = jnp.arange(experts * capacity, dtype=jnp.int32)
    by_route = slot_lines[:, None] == slot_index[None, :]
    by_token = jnp.any(by_route.reshape(experts * capacity, tok_count, top_count), axis=2)
    return (by_route, by_token)


def columns(array, part, parts):
    width = array.shape[1] // parts
    return array[:, part * width : (part + 1) * width]


def shards(tokens, out_grad, route_ids, route_weights, gate_proj, up_proj, down_proj):
    node_count = lax.axis_size("node")
    local_count = lax.axis_size("local")
    tok_count, top_count = route_ids.shape
    capacity = max(2, 3 * tok_count * top_count // (2 * node_count))
    by_route, by_token = slot_tables(route_ids, node_count, capacity)
    token_mask = by_token.astype(jnp.bfloat16)
    weight_line = route_weights.reshape(1, tok_count * top_count).astype(jnp.float32)
    send_g = jnp.sum(jnp.where(by_route, weight_line, 0.0), axis=1).astype(jnp.bfloat16)

    def spread(rows):
        near = lax.all_to_all(rows, "node", split_axis=0, concat_axis=0, tiled=True)
        return lax.all_gather(near, "local", axis=0, tiled=True)

    def collect(rows):
        near = lax.psum_scatter(rows, "local", scatter_dimension=0, tiled=True)
        return lax.all_to_all(near, "node", split_axis=0, concat_axis=0, tiled=True)

    def dispatch(array):
        return [
            spread(
                jnp.dot(
                    token_mask, columns(array, c, IN_PARTS), preferred_element_type=jnp.float32
                ).astype(jnp.bfloat16)
            )
            for c in range(IN_PARTS)
        ]

    rows_x = dispatch(tokens)
    rows_g = spread(send_g.reshape(node_count, capacity)).reshape(-1)
    rows_dy = dispatch(out_grad)
    gate_w = gate_proj[0]
    up_w = up_proj[0]
    down_w = down_proj[0]
    width = gate_w.shape[0] // IN_PARTS
    pre_gate = sum(
        jnp.dot(r, gate_w[c * width : (c + 1) * width], preferred_element_type=jnp.float32)
        for c, r in enumerate(rows_x)
    )
    pre_up = sum(
        jnp.dot(r, up_w[c * width : (c + 1) * width], preferred_element_type=jnp.float32)
        for c, r in enumerate(rows_x)
    )
    gate_sigmoid = jax.nn.sigmoid(pre_gate)
    gate_silu = pre_gate * gate_sigmoid
    activated = (gate_silu * pre_up).astype(jnp.bfloat16)
    columns_both = (((1,), (1,)), ((), ()))
    back_proj = sum(
        lax.dot_general(
            r, columns(down_w, c, IN_PARTS), columns_both, preferred_element_type=jnp.float32
        )
        for c, r in enumerate(rows_dy)
    )
    gate_scale = rows_g.astype(jnp.float32)[:, None]
    grad_act = gate_scale * back_proj
    grad_pregate = (
        grad_act * pre_up * gate_sigmoid * (1.0 + pre_gate * (1.0 - gate_sigmoid))
    ).astype(jnp.bfloat16)
    grad_preup = (grad_act * gate_silu).astype(jnp.bfloat16)
    part_g = jnp.sum(activated.astype(jnp.float32) * back_proj, axis=1)
    width = gate_w.shape[0] // OUT_PARTS
    got_x = []
    for c in range(OUT_PARTS):
        part_x = lax.dot_general(
            grad_pregate, gate_w[c * width : (c + 1) * width], columns_both,
            preferred_element_type=jnp.float32,
        )
        part_x = part_x + lax.dot_general(
            grad_preup, up_w[c * width : (c + 1) * width], columns_both,
            preferred_element_type=jnp.float32,
        )
        got_x.append(collect(part_x.astype(jnp.bfloat16)))
    got_g = collect(part_g.reshape(local_count * node_count, capacity)).reshape(-1)
    rows_first = (((0,), (0,)), ((), ()))
    grad_gate = jnp.concatenate(
        [
            lax.dot_general(
                r, grad_pregate, rows_first, preferred_element_type=jnp.float32
            ).astype(jnp.bfloat16)
            for r in rows_x
        ]
    )
    grad_up = jnp.concatenate(
        [
            lax.dot_general(
                r, grad_preup, rows_first, preferred_element_type=jnp.float32
            ).astype(jnp.bfloat16)
            for r in rows_x
        ]
    )
    grad_down = jnp.concatenate(
        [
            lax.dot_general(
                activated,
                (gate_scale * r.astype(jnp.float32)).astype(jnp.bfloat16),
                rows_first,
                preferred_element_type=jnp.float32,
            ).astype(jnp.bfloat16)
            for r in rows_dy
        ],
        axis=1,
    )
    grad_tokens = jnp.concatenate(
        [
            lax.dot_general(
                token_mask, got, rows_first, preferred_element_type=jnp.float32
            ).astype(jnp.bfloat16)
            for got in got_x
        ],
        axis=1,
    )
    grad_routes = jnp.sum(jnp.where(by_route, got_g[:, None], 0.0), axis=0).reshape(
        tok_count, top_count
    )
    return (
        grad_tokens,
        grad_routes,
        grad_gate.reshape(gate_proj.shape),
        grad_up.reshape(up_proj.shape),
        grad_down.reshape(down_proj.shape),
    )


def solution(mesh):
    token_spec = P(("node", "local"), None)
    wide_spec = P("node", None, "local")
    tall_spec = P("node", "local", None)
    return jax.shard_map(
        shards,
        mesh=mesh,
        in_specs=(token_spec,) * 4 + (wide_spec, wide_spec, tall_spec),
        out_specs=(token_spec, token_spec, wide_spec, wide_spec, tall_spec),
        check_vma=False,
    )
```

```python
import jax
import jax.numpy as jnp
from jax import lax
from jax.sharding import PartitionSpec as P

X_CUTS = (0, 2, 4)
DY_CUTS = (0, 2, 3, 4)
OUT_PARTS = 4
LANES = 128


def slot_tables(route_ids, experts, capacity):
    tok_count, top_count = route_ids.shape
    flat_ids = route_ids.reshape(tok_count * top_count)
    route_order = jnp.arange(tok_count * top_count, dtype=jnp.int32)
    same_ids = (flat_ids[:, None] == flat_ids[None, :]) & (
        route_order[None, :] < route_order[:, None]
    )
    rank_ids = jnp.sum(same_ids.astype(jnp.int32), axis=1)
    slot_index = flat_ids * capacity + rank_ids
    slot_lines = jnp.arange(experts * capacity, dtype=jnp.int32)
    by_route = slot_lines[:, None] == slot_index[None, :]
    by_token = jnp.any(by_route.reshape(experts * capacity, tok_count, top_count), axis=2)
    return (by_route, by_token)


def shards(tokens, out_grad, route_ids, route_weights, gate_proj, up_proj, down_proj):
    node_count = lax.axis_size("node")
    local_count = lax.axis_size("local")
    tok_count, top_count = route_ids.shape
    capacity = max(2, 3 * tok_count * top_count // (2 * node_count))
    by_route, by_token = slot_tables(route_ids, node_count, capacity)
    token_mask = by_token.astype(jnp.bfloat16)
    weight_line = route_weights.reshape(1, tok_count * top_count).astype(jnp.float32)
    send_g = jnp.sum(jnp.where(by_route, weight_line, 0.0), axis=1).astype(jnp.bfloat16)
    send_g = jnp.broadcast_to(send_g[:, None], (node_count * capacity, LANES))

    def swap(rows, bit):
        pairs = [(i, i ^ bit) for i in range(local_count)]
        return lax.ppermute(rows, "local", pairs)

    def spread(rows):
        rows = lax.all_to_all(rows, "node", split_axis=0, concat_axis=0, tiled=True)
        bit = 2
        while bit < local_count:
            rows = jnp.concatenate([rows, swap(rows, bit)])
            bit = 2 * bit
        return jnp.concatenate([rows, swap(rows, 1)])

    def collect(rows):
        for bit in [1] + [local_count >> k for k in range(1, local_count.bit_length() - 1)]:
            keep, give = jnp.split(rows, 2)
            got = swap(give, bit)
            rows = (keep.astype(jnp.float32) + got.astype(jnp.float32)).astype(jnp.bfloat16)
        return lax.all_to_all(rows, "node", split_axis=0, concat_axis=0, tiled=True)

    unit = tokens.shape[1] // X_CUTS[-1]
    x_spans = [(a * unit, b * unit) for a, b in zip(X_CUTS, X_CUTS[1:])]
    dy_spans = [(a * unit, b * unit) for a, b in zip(DY_CUTS, DY_CUTS[1:])]

    def pick(array, span):
        part = array[:, span[0] : span[1]]
        rows = jnp.dot(token_mask, part, preferred_element_type=jnp.float32)
        return rows.astype(jnp.bfloat16)

    first_rows = spread(jnp.concatenate([pick(tokens, x_spans[0]), send_g], axis=1))
    rows_g = first_rows[:, -1]
    rows_x = [first_rows[:, :-LANES]] + [spread(pick(tokens, span)) for span in x_spans[1:]]
    rows_dy = [spread(pick(out_grad, span)) for span in dy_spans]
    gate_w = gate_proj[0]
    up_w = up_proj[0]
    down_w = down_proj[0]
    pre_gate = sum(
        jnp.dot(r, gate_w[a:b], preferred_element_type=jnp.float32)
        for (a, b), r in zip(x_spans, rows_x)
    )
    pre_up = sum(
        jnp.dot(r, up_w[a:b], preferred_element_type=jnp.float32)
        for (a, b), r in zip(x_spans, rows_x)
    )
    gate_sigmoid = jax.nn.sigmoid(pre_gate)
    gate_silu = pre_gate * gate_sigmoid
    activated = (gate_silu * pre_up).astype(jnp.bfloat16)
    columns_both = (((1,), (1,)), ((), ()))
    back_proj = sum(
        lax.dot_general(
            r, down_w[:, a:b], columns_both, preferred_element_type=jnp.float32
        )
        for (a, b), r in zip(dy_spans, rows_dy)
    )
    gate_scale = rows_g.astype(jnp.float32)[:, None]
    grad_act = gate_scale * back_proj
    grad_pregate = (
        grad_act * pre_up * gate_sigmoid * (1.0 + pre_gate * (1.0 - gate_sigmoid))
    ).astype(jnp.bfloat16)
    grad_preup = (grad_act * gate_silu).astype(jnp.bfloat16)
    part_g = jnp.sum(activated.astype(jnp.float32) * back_proj, axis=1)
    width = gate_w.shape[0] // OUT_PARTS
    got_x = []
    for c in range(OUT_PARTS):
        part_x = lax.dot_general(
            grad_pregate, gate_w[c * width : (c + 1) * width], columns_both,
            preferred_element_type=jnp.float32,
        )
        part_x = part_x + lax.dot_general(
            grad_preup, up_w[c * width : (c + 1) * width], columns_both,
            preferred_element_type=jnp.float32,
        )
        part_x = part_x.astype(jnp.bfloat16)
        if c == OUT_PARTS - 1:
            lanes_g = jnp.broadcast_to(part_g.astype(jnp.bfloat16)[:, None], (part_g.shape[0], LANES))
            part_x = jnp.concatenate([part_x, lanes_g], axis=1)
        got_x.append(collect(part_x))
    got_g = got_x[-1][:, -1].astype(jnp.float32)
    got_x[-1] = got_x[-1][:, :-LANES]
    rows_first = (((0,), (0,)), ((), ()))
    grad_gate = jnp.concatenate(
        [
            lax.dot_general(
                r, grad_pregate, rows_first, preferred_element_type=jnp.float32
            ).astype(jnp.bfloat16)
            for r in rows_x
        ]
    )
    grad_up = jnp.concatenate(
        [
            lax.dot_general(
                r, grad_preup, rows_first, preferred_element_type=jnp.float32
            ).astype(jnp.bfloat16)
            for r in rows_x
        ]
    )
    grad_down = jnp.concatenate(
        [
            lax.dot_general(
                activated,
                (gate_scale * r.astype(jnp.float32)).astype(jnp.bfloat16),
                rows_first,
                preferred_element_type=jnp.float32,
            ).astype(jnp.bfloat16)
            for r in rows_dy
        ],
        axis=1,
    )
    grad_tokens = jnp.concatenate(
        [
            lax.dot_general(
                token_mask, got, rows_first, preferred_element_type=jnp.float32
            ).astype(jnp.bfloat16)
            for got in got_x
        ],
        axis=1,
    )
    grad_routes = jnp.sum(jnp.where(by_route, got_g[:, None], 0.0), axis=0).reshape(
        tok_count, top_count
    )
    return (
        grad_tokens,
        grad_routes,
        grad_gate.reshape(gate_proj.shape),
        grad_up.reshape(up_proj.shape),
        grad_down.reshape(down_proj.shape),
    )


def solution(mesh):
    token_spec = P(("node", "local"), None)
    wide_spec = P("node", None, "local")
    tall_spec = P("node", "local", None)
    return jax.shard_map(
        shards,
        mesh=mesh,
        in_specs=(token_spec,) * 4 + (wide_spec, wide_spec, tall_spec),
        out_specs=(token_spec, token_spec, wide_spec, wide_spec, tall_spec),
        check_vma=False,
    )
```
